32 devices in a mesh: ctx: 8 (over z, x), dp: 4 (over y, core).
Axes of the slice: x: 2, y: 2, z: 4, core: 2. Of those that a mesh axis runs over, the one named last changes fastest.
Arguments:
- recurrent_probe_vectors: bfloat16 [4096, 4096], P(('dp', 'ctx')), parts along dimension 0, may hold values from -3 to 3
- recurrent_matcher_vectors: bfloat16 [4096, 4096], P(('dp', 'ctx')), parts along dimension 0, may hold values from -3 to 3
- recurrent_content_vectors: bfloat16 [4096, 4096], P(('dp', 'ctx')), parts along dimension 0, may hold values from -6 to 6
- recurrent_result_sensitivity: bfloat16 [4096, 4096], P(('dp', 'ctx')), parts along dimension 0, may hold values from -6 to 6
- attender_fade_power: int32 [128], P('dp'), parts along dimension 0, may hold values from 5 to 16
- surplus_fade_amounts: float32 [4096, 32], P(('dp', 'ctx')), parts along dimension 0, may hold values from -0.7 to 0
- normalized_probe_vectors: bfloat16 [4096, 4096], P(('dp', 'ctx')), parts along dimension 0, may hold values from -120 to 120
- normalized_matcher_vectors: bfloat16 [4096, 512], P(('dp', 'ctx')), parts along dimension 0, may hold values from -5 to 5
- normalized_content_vectors: bfloat16 [4096, 512], P(('dp', 'ctx')), parts along dimension 0, may hold values from -6 to 6
- normalized_result_sensitivity: bfloat16 [4096, 4096], P(('dp', 'ctx')), parts along dimension 0, may hold values from -6 to 6
Outputs:
- linear_query_grad: bfloat16 [4096, 4096], P(('dp', 'ctx')), parts along dimension 0
- linear_key_grad: bfloat16 [4096, 4096], P(('dp', 'ctx')), parts along dimension 0
- linear_value_grad: bfloat16 [4096, 4096], P(('dp', 'ctx')), parts along dimension 0
- softmax_query_grad: bfloat16 [4096, 4096], P(('dp', 'ctx')), parts along dimension 0
- softmax_key_grad: bfloat16 [4096, 512], P(('dp', 'ctx')), parts along dimension 0
- softmax_value_grad: bfloat16 [4096, 512], P(('dp', 'ctx')), parts along dimension 0
The draws below stay inside these ranges and needn't reach their ends.
There are 4 independent parts, one for each index of `dp`. The reference program is written for one: setup_inputs(seed, part) draws one part's arguments, and reference() takes and returns one part's arrays. A program takes and returns all parts, laid end to end along the dimension named above; each array names one. Nothing has to cross between parts.
All inputs are finite; a program needn't handle non-finite values.
Results may differ from the reference program's by a relative error of at most 0.012.
Values may be sent and summed in bfloat16 or wider, within the bound.
A program may use at most 128 MiB of HBM per device.

```python
import jax
import jax.numpy as jnp
from jax import lax

H = 32
HD = 128
G = 4
TOK_DEV = 128
WIN_DEV = 3
SEQ = 1024
N_CTX = 8


def softmax_pair(key):
    base = jax.random.fold_in(key, 4242)
    key_query, key_keys = jax.random.split(base, 2)
    query = jnp.clip(jax.random.normal(key_query, (SEQ, H * HD), jnp.float32), -5.0, 5.0)
    keys = jnp.clip(jax.random.normal(key_keys, (SEQ, G * HD), jnp.float32), -5.0, 5.0)
    return (query, keys)


def draw_normalized_probe_vectors(key, part):
    return softmax_pair(key)[0].astype(jnp.bfloat16)


def draw_normalized_matcher_vectors(key, part):
    return softmax_pair(key)[1].astype(jnp.bfloat16)


def draw_surplus_fade_amounts(key, part):
    base = jax.random.fold_in(key, 77)
    key_hits, key_sizes = jax.random.split(base)
    hits = jax.random.bernoulli(key_hits, 4.0 / SEQ, (SEQ, H))
    sizes = jnp.log(jax.random.uniform(key_sizes, (SEQ, H), jnp.float32, 0.5, 0.8))
    return jnp.where(hits, sizes, 0.0).astype(jnp.float32)


def set_ends(result, own_key, low, largest):
    spot = [jax.random.randint(jax.random.fold_in(own_key, axis), (), 0, length) for axis, length in enumerate(result.shape)]
    longest = result.shape.index(max(result.shape))
    neighbour = spot[:longest] + [(spot[longest] + 1) % result.shape[longest]] + spot[longest + 1:]
    return result.at[tuple(spot)].set(low).at[tuple(neighbour)].set(largest)


def block_scale(rng, dims, shards, smallest, top_value):
    factor_of = 1.0
    for dim, parts in shards:
        steps = jax.random.uniform(jax.random.fold_in(jax.random.fold_in(rng, 6), dim), (parts,), jnp.float32, smallest / len(shards), top_value / len(shards))
        factor_of = factor_of * jnp.repeat(jnp.exp(steps), dims[dim] // parts).reshape((-1,) + (1,) * (len(dims) - 1 - dim))
    return factor_of


def centred(own_key, dims, scale, bound, cuts=(), kind=jnp.bfloat16):
    entries = jax.random.normal(own_key, dims, jnp.float32) * scale
    if len(cuts) > 0:
        entries = block_scale(own_key, dims, cuts, -0.22, 0.18) * entries
    return jnp.clip(entries, min=-bound, max=bound).astype(kind)


def setup_inputs(seed: int = 0, part: int = 0) -> dict:
    splits = jax.random.split(jax.random.key(seed), 11)
    own_keys = jax.random.split(jax.random.fold_in(splits[10], part), 11)
    return {
        "recurrent_probe_vectors": centred(own_keys[0], (SEQ, H * HD), 0.5, 3.0, ((0, 8),)),
        "recurrent_matcher_vectors": centred(own_keys[1], (SEQ, H * HD), 0.5, 3.0, ((0, 8),)),
        "recurrent_content_vectors": centred(own_keys[2], (SEQ, H * HD), 1.0, 6.0, ((0, 8),)),
        "recurrent_result_sensitivity": centred(own_keys[3], (SEQ, H * HD), 1.0, 6.0, ((0, 8),)),
        "attender_fade_power": set_ends(jax.random.randint(own_keys[4], (H,), 5, 17), jax.random.fold_in(own_keys[4], 1), 5, 16).astype(jnp.int32),
        "surplus_fade_amounts": draw_surplus_fade_amounts(jax.random.fold_in(jax.random.fold_in(splits[10], part), 71), part),
        "normalized_probe_vectors": draw_normalized_probe_vectors(jax.random.fold_in(jax.random.fold_in(splits[10], part), 71), part),
        "normalized_matcher_vectors": draw_normalized_matcher_vectors(jax.random.fold_in(jax.random.fold_in(splits[10], part), 71), part),
        "normalized_content_vectors": centred(own_keys[8], (SEQ, G * HD), 1.0, 6.0, ((0, 8),)),
        "normalized_result_sensitivity": centred(own_keys[9], (SEQ, H * HD), 1.0, 6.0, ((0, 8),)),
    }


def linear_local(query, keys, values, cotangent, fade_natural_rate):
    tokens = query.shape[0]
    number_of_attenders = fade_natural_rate.shape[1]
    width = query.shape[1] // number_of_attenders
    scale = 1.0 / width
    query_three = query.reshape(tokens, number_of_attenders, width).astype(jnp.float32)
    keys_three = keys.reshape(tokens, number_of_attenders, width).astype(jnp.float32)
    values_three = values.reshape(tokens, number_of_attenders, width).astype(jnp.float32)
    cotan_three = cotangent.reshape(tokens, number_of_attenders, width).astype(jnp.float32)
    cumul = jnp.cumsum(fade_natural_rate, axis=0)
    total = cumul[-1]
    heads_cumul = cumul.T
    spread = heads_cumul[:, :, None] - heads_cumul[:, None, :]
    causal = lax.broadcasted_iota(jnp.int32, (tokens, tokens), 0) >= lax.broadcasted_iota(jnp.int32, (tokens, tokens), 1)
    decay = jnp.where(causal[None], jnp.exp(jnp.minimum(spread, 0.0)), 0.0)
    outer_grad = jnp.einsum('thd,shd->hts', cotan_three, values_three)
    outer_score = jnp.einsum('thd,shd->hts', query_three, keys_three)
    mix_grad = (decay * outer_grad * scale).astype(jnp.bfloat16).astype(jnp.float32)
    mix_score = (decay * outer_score * scale).astype(jnp.bfloat16).astype(jnp.float32)
    inner_query = jnp.einsum('hts,shd->thd', mix_grad, keys_three)
    inner_key = jnp.einsum('hts,thd->shd', mix_grad, query_three)
    inner_value = jnp.einsum('hts,thd->shd', mix_score, cotan_three)
    to_end = jnp.exp(total[None, :] - cumul)
    from_start = jnp.exp(cumul)
    weighted_key = (keys_three * to_end[:, :, None]).astype(jnp.bfloat16).astype(jnp.float32)
    weighted_query = (query_three * from_start[:, :, None]).astype(jnp.bfloat16).astype(jnp.float32)
    key_state = jnp.einsum('shd,she->hde', weighted_key, values_three)
    grad_state = jnp.einsum('thd,the->hde', weighted_query, cotan_three)
    return inner_query, inner_key, inner_value, key_state, grad_state, total, to_end, from_start


def linear_finish(inner_query, inner_key, inner_value, key_in, grad_in, to_end, from_start, keys, values, cotangent):
    tokens, number_of_attenders, width = inner_query.shape
    scale = 1.0 / width
    keys_three = keys.reshape(tokens, number_of_attenders, width).astype(jnp.float32)
    values_three = values.reshape(tokens, number_of_attenders, width).astype(jnp.float32)
    cotan_three = cotangent.reshape(tokens, number_of_attenders, width).astype(jnp.float32)
    key_half = key_in.astype(jnp.bfloat16).astype(jnp.float32)
    grad_half = grad_in.astype(jnp.bfloat16).astype(jnp.float32)
    query_grad = inner_query + scale * from_start[:, :, None] * jnp.einsum('hde,the->thd', key_half, cotan_three)
    key_grad = inner_key + scale * to_end[:, :, None] * jnp.einsum('hde,she->shd', grad_half, values_three)
    value_grad = inner_value + scale * to_end[:, :, None] * jnp.einsum('hde,shd->she', grad_half, keys_three)
    flat = tokens, number_of_attenders * width
    return (query_grad.reshape(flat).astype(jnp.bfloat16), key_grad.reshape(flat).astype(jnp.bfloat16),
            value_grad.reshape(flat).astype(jnp.bfloat16))


def combine_states(earlier, later):
    return (later[0] + jnp.exp(later[1])[:, None, None] * earlier[0], earlier[1] + later[1])


def softmax_block(query, cotangent, keys, values, visible, groups):
    rows = query.shape[0]
    width = keys.shape[1] // groups
    number_of_attenders = query.shape[1] // width
    share = number_of_attenders // groups
    scale = width ** -0.5
    query_groups = query.reshape(rows, groups, share, width).transpose(1, 0, 2, 3)
    cotan_groups = cotangent.reshape(rows, groups, share, width).transpose(1, 0, 2, 3)
    key_groups = keys.reshape(-1, groups, width).transpose(1, 0, 2)
    value_groups = values.reshape(-1, groups, width).transpose(1, 0, 2)

    def one_group(pieces):
        query_head, cotan_head, key_head, value_head = [piece.astype(jnp.float32) for piece in pieces]
        score = jnp.einsum('trd,sd->rts', query_head, key_head) * scale
        score = jnp.where(visible[None], score, -jnp.inf)
        peak = jnp.max(score, axis=2, keepdims=True)
        expo = jnp.exp(score - peak)
        prob = expo / jnp.sum(expo, axis=2, keepdims=True)
        prob_half = prob.astype(jnp.bfloat16).astype(jnp.float32)
        output = jnp.einsum('rts,se->tre', prob_half, value_head).astype(jnp.bfloat16)
        output = lax.optimization_barrier(output)
        delta = jnp.sum(cotan_head * output.astype(jnp.float32), axis=2)
        dprob = jnp.einsum('tre,se->rts', cotan_head, value_head)
        dscore = prob * (dprob - delta.T[:, :, None])
        dscore_half = dscore.astype(jnp.bfloat16).astype(jnp.float32)
        query_grad = jnp.einsum('rts,sd->trd', dscore_half, key_head) * scale
        key_grad = jnp.einsum('rts,trd->sd', dscore_half, query_head) * scale
        value_grad = jnp.einsum('rts,tre->se', prob_half, cotan_head)
        return query_grad, key_grad, value_grad

    query_grad, key_grad, value_grad = lax.map(one_group, (query_groups, cotan_groups, key_groups, value_groups))
    query_grad = query_grad.transpose(1, 0, 2, 3).reshape(rows, number_of_attenders * width)
    key_grad = key_grad.transpose(1, 0, 2).reshape(-1, groups * width)
    value_grad = value_grad.transpose(1, 0, 2).reshape(-1, groups * width)
    return query_grad, key_grad, value_grad


def reference(recurrent_probe_vectors, recurrent_matcher_vectors, recurrent_content_vectors, recurrent_result_sensitivity, attender_fade_power, surplus_fade_amounts,
              normalized_probe_vectors, normalized_matcher_vectors, normalized_content_vectors, normalized_result_sensitivity):
    blocks = N_CTX
    rows = TOK_DEV
    fade_natural_rate = surplus_fade_amounts - jnp.power(2.0, -attender_fade_power.astype(jnp.float32))[None, :]
    split_rows = lambda array: array.reshape(blocks, rows, array.shape[1])
    locals_all = lax.map(lambda pieces: linear_local(*pieces),
                         (split_rows(recurrent_probe_vectors), split_rows(recurrent_matcher_vectors), split_rows(recurrent_content_vectors),
                          split_rows(recurrent_result_sensitivity), split_rows(fade_natural_rate)))
    inner_query, inner_key, inner_value, key_state, grad_state, total, to_end, from_start = locals_all
    start = (jnp.zeros((H, HD, HD), jnp.float32), jnp.zeros((H,), jnp.float32))

    def carry_step(carry, item):
        return combine_states(carry, item), carry

    _, (key_in, _) = lax.scan(carry_step, start, (key_state, total))
    _, (grad_in, _) = lax.scan(carry_step, start, (grad_state, total), reverse=True)
    grads = lax.map(lambda pieces: linear_finish(*pieces),
                    (inner_query, inner_key, inner_value, key_in, grad_in, to_end, from_start,
                     split_rows(recurrent_matcher_vectors), split_rows(recurrent_content_vectors), split_rows(recurrent_result_sensitivity)))
    linear_query_grad = grads[0].reshape(SEQ, H * HD)
    linear_key_grad = grads[1].reshape(SEQ, H * HD)
    linear_value_grad = grads[2].reshape(SEQ, H * HD)

    margin = (WIN_DEV - 1) * rows
    span = WIN_DEV * rows
    key_padded = jnp.concatenate([jnp.zeros((margin, G * HD), normalized_matcher_vectors.dtype), normalized_matcher_vectors], axis=0)
    value_padded = jnp.concatenate([jnp.zeros((margin, G * HD), normalized_content_vectors.dtype), normalized_content_vectors], axis=0)
    positions = lax.broadcasted_iota(jnp.int32, (span,), 0)
    query_pos = lax.broadcasted_iota(jnp.int32, (rows,), 0)

    def per_block(carry, block):
        key_acc, value_acc = carry
        first = (block * rows).astype(jnp.int32)
        query_block = lax.dynamic_slice_in_dim(normalized_probe_vectors, first, rows, 0)
        cotan_block = lax.dynamic_slice_in_dim(normalized_result_sensitivity, first, rows, 0)
        key_block = lax.dynamic_slice_in_dim(key_padded, first, span, 0)
        value_block = lax.dynamic_slice_in_dim(value_padded, first, span, 0)
        owner = block - WIN_DEV + 1 + positions // rows
        within = positions % rows
        visible = (owner >= 0)[None, :] & ((owner < block)[None, :] | (within[None, :] <= query_pos[:, None]))
        query_grad, key_grad, value_grad = softmax_block(query_block, cotan_block, key_block, value_block, visible, G)
        key_acc = lax.dynamic_update_slice_in_dim(key_acc, lax.dynamic_slice_in_dim(key_acc, first, span, 0) + key_grad, first, 0)
        value_acc = lax.dynamic_update_slice_in_dim(value_acc, lax.dynamic_slice_in_dim(value_acc, first, span, 0) + value_grad, first, 0)
        return (key_acc, value_acc), query_grad.astype(jnp.bfloat16)

    zeros = jnp.zeros((SEQ + margin, G * HD), jnp.float32)
    (key_acc, value_acc), query_grads = lax.scan(per_block, (zeros, zeros), jnp.arange(blocks, dtype=jnp.int32))
    softmax_query_grad = query_grads.reshape(SEQ, H * HD)
    softmax_key_grad = key_acc[margin:].astype(jnp.bfloat16)
    softmax_value_grad = value_acc[margin:].astype(jnp.bfloat16)
    return (linear_query_grad, linear_key_grad, linear_value_grad,
            softmax_query_grad, softmax_key_grad, softmax_value_grad)
```

```python
import functools

import jax
import jax.numpy as jnp
from jax import lax
from jax.experimental import pallas as pl
from jax.experimental.pallas import tpu as pltpu
from jax.sharding import PartitionSpec as P

G = 4
WINDOW = 3
CH = 2
LAG = 1
SOFT_DELAY = 2
F32 = jnp.float32
BF16 = jnp.bfloat16


def dot(a, b, ca, cb):
    return lax.dot_general(a, b, (((ca,), (cb,)), ((), ())), preferred_element_type=F32)


def kernel(
    n,
    q_ref,
    k_ref,
    v_ref,
    do_ref,
    cum_ref,
    sq_ref,
    sk_ref,
    sv_ref,
    sdo_ref,
    lq_out,
    lk_out,
    lv_out,
    sq_out,
    sk_out,
    sv_out,
    mg_s,
    ms_s,
    ks_s,
    gs_s,
    fin,
    fout,
    gin,
    gout,
    kvin,
    kcat,
    vcat,
    acc,
    gland,
    fsend,
    frecv,
    bsend,
    brecv,
    kvsend,
    kvrecv,
    gsend,
    grecv,
):
    T = q_ref.shape[0]
    D = T
    H = cum_ref.shape[0]
    NC = H // CH
    share = H // G
    per_group = share // CH
    me = lax.axis_index("ctx")
    scale = 1.0 / D
    sscale = D ** (-0.5)

    def there(offset):
        return (me + offset >= 0) & (me + offset < n)

    def device(offset):
        if offset > 0:
            return {"ctx": jnp.where(me + offset < n, me + offset, me - offset)}
        return {"ctx": jnp.where(me + offset >= 0, me + offset, me - offset)}

    def remote(src, dst, send, recv, offset):
        return pltpu.make_async_remote_copy(
            src_ref=src,
            dst_ref=dst,
            send_sem=send,
            recv_sem=recv,
            device_id=device(offset),
            device_id_type=pl.DeviceIdType.MESH,
        )

    def fwd_copy(c):
        part = pl.ds(c * CH, CH)
        return remote(fout.at[part], fin.at[part], fsend.at[c], frecv.at[c], 1)

    def bwd_copy(c):
        part = pl.ds(c * CH, CH)
        return remote(gout.at[part], gin.at[part], bsend.at[c], brecv.at[c], -1)

    def kv_copy(slot, which):
        src = sk_ref if which == 0 else sv_ref
        i = slot * 2 + which
        return remote(src, kvin.at[slot, which], kvsend.at[i], kvrecv.at[i], slot + 1)

    def grad_copy(slot, g):
        return remote(
            acc.at[slot + 1, g], gland.at[slot, g], gsend.at[slot, g], grecv.at[slot, g], -(slot + 1)
        )

    barrier = pltpu.get_barrier_semaphore()
    for offset in (-2, -1, 1, 2):

        @pl.when(there(offset))
        def _():
            pl.semaphore_signal(
                barrier, inc=1, device_id=device(offset), device_id_type=pl.DeviceIdType.MESH
            )

    peers = jnp.minimum(me, 2) + jnp.minimum(n - 1 - me, 2)
    pl.semaphore_wait(barrier, peers)

    for slot in range(2):

        @pl.when(there(slot + 1))
        def _():
            kv_copy(slot, 0).start()
            kv_copy(slot, 1).start()

        @pl.when(jnp.logical_not(there(-slot - 1)))
        def _():
            kvin[slot] = jnp.zeros(kvin.shape[1:], BF16)

        @pl.when(jnp.logical_not(there(slot + 1)))
        def _():
            gland[slot] = jnp.zeros(gland.shape[1:], F32)

    @pl.when(me == 0)
    def _():
        fin[...] = jnp.zeros(fin.shape, BF16)

    @pl.when(me == n - 1)
    def _():
        gin[...] = jnp.zeros(gin.shape, BF16)

    acc[...] = jnp.zeros(acc.shape, F32)

    rows_i = lax.broadcasted_iota(jnp.int32, (T, T), 0)
    cols_i = lax.broadcasted_iota(jnp.int32, (T, T), 1)

    def cols(h):
        return pl.ds(pl.multiple_of(h * D, D), D)

    def fades(h):
        row = cum_ref[h]
        wide = jnp.broadcast_to(row, (T, T))
        tall = wide.T
        return row[:, T - 1 : T], wide, tall

    def local(c):
        for j in range(CH):
            h = c * CH + j
            at = cols(h)
            total, wide, tall = fades(h)
            decay = jnp.where(rows_i >= cols_i, jnp.exp(jnp.minimum(tall - wide, 0.0)), 0.0)
            q, k, v, do = q_ref[:, at], k_ref[:, at], v_ref[:, at], do_ref[:, at]
            wk = (k.astype(F32) * jnp.exp(total - tall)).astype(BF16)
            wq = (q.astype(F32) * jnp.exp(tall)).astype(BF16)
            ks_s[h] = dot(wk, v, 0, 0)
            gs_s[h] = dot(wq, do, 0, 0)
            mg_s[h] = (decay * dot(do, v, 1, 1) * scale).astype(BF16)
            ms_s[h] = (decay * dot(q, k, 1, 1) * scale).astype(BF16)

    def pass_state(c, state, arrived, out):
        for j in range(CH):
            h = c * CH + j
            row = cum_ref[h]
            out[h] = (state[h] + jnp.exp(row[:, T - 1 : T]) * arrived[h].astype(F32)).astype(BF16)

    def fwd_pass(c):
        @pl.when(there(-1))
        def _():
            fwd_copy(c).wait_recv()

        @pl.when(there(1))
        def _():
            pass_state(c, ks_s, fin, fout)
            fwd_copy(c).start()

    def bwd_pass(c):
        @pl.when(there(1))
        def _():
            bwd_copy(c).wait_recv()

        @pl.when(there(-1))
        def _():
            pass_state(c, gs_s, gin, gout)
            bwd_copy(c).start()

    def fwd_finish(c):
        for j in range(CH):
            h = c * CH + j
            at = cols(h)
            total, wide, tall = fades(h)
            inner = dot(mg_s[h], k_ref[:, at], 1, 0)
            outer = dot(do_ref[:, at], fin[h], 1, 1)
            lq_out[:, at] = (inner + scale * jnp.exp(tall) * outer).astype(BF16)

    def bwd_finish(c):
        for j in range(CH):
            h = c * CH + j
            at = cols(h)
            total, wide, tall = fades(h)
            to_end = scale * jnp.exp(total - tall)
            lk_out[:, at] = (
                dot(mg_s[h], q_ref[:, at], 0, 0) + to_end * dot(v_ref[:, at], gin[h], 1, 1)
            ).astype(BF16)
            lv_out[:, at] = (
                dot(ms_s[h], do_ref[:, at], 0, 0) + to_end * dot(k_ref[:, at], gin[h], 1, 0)
            ).astype(BF16)

    def soft_begin():
        for slot in range(2):

            @pl.when(there(-slot - 1))
            def _():
                kv_copy(slot, 0).wait_recv()
                kv_copy(slot, 1).wait_recv()

        for g in range(G):
            at = slice(g * D, (g + 1) * D)
            kcat[g, 0:T] = sk_ref[:, at]
            vcat[g, 0:T] = sv_ref[:, at]
            for slot in range(2):
                kcat[g, (slot + 1) * T : (slot + 2) * T] = kvin[slot, 0, :, at]
                vcat[g, (slot + 1) * T : (slot + 2) * T] = kvin[slot, 1, :, at]

    span = WINDOW * T

    def soft(c):
        g = c // per_group
        k, v = kcat[g], vcat[g]
        q = jnp.concatenate([sq_ref[:, cols(c * CH + j)] for j in range(CH)], axis=0)
        do = jnp.concatenate([sdo_ref[:, cols(c * CH + j)] for j in range(CH)], axis=0)
        t = lax.broadcasted_iota(jnp.int32, (CH * T, span), 0) % T
        s = lax.broadcasted_iota(jnp.int32, (CH * T, span), 1)
        visible = (s <= t) | ((s >= T) & (s < (me + 1) * T))
        score = jnp.where(visible, dot(q, k, 1, 1) * sscale, -jnp.inf)
        peak = jnp.max(score, axis=1, keepdims=True)
        expo = jnp.exp(score - peak)
        prob = expo * (1.0 / jnp.sum(expo, axis=1, keepdims=True))
        half = prob.astype(BF16)
        out = dot(half, v, 1, 0).astype(BF16)
        delta = jnp.sum(do.astype(F32) * out.astype(F32), axis=1, keepdims=True)
        ds = (prob * (dot(do, v, 1, 1) - delta)).astype(BF16)
        dq = (dot(ds, k, 1, 0) * sscale).astype(BF16)
        for j in range(CH):
            sq_out[:, cols(c * CH + j)] = dq[j * T : (j + 1) * T]
        dk = dot(ds, q, 0, 0) * sscale
        dv = dot(half, do, 0, 0)
        for slot in range(WINDOW):
            acc[slot, g, 0] += dk[slot * T : (slot + 1) * T]
            acc[slot, g, 1] += dv[slot * T : (slot + 1) * T]

        @pl.when(c % per_group == per_group - 1)
        def _():
            for slot in range(2):

                @pl.when(there(-slot - 1))
                def _():
                    grad_copy(slot, g).start()

    def step(s, carry):
        cf = s - LAG * me
        cb = s - LAG * (n - 1 - me)
        cs = s - SOFT_DELAY
        on_f = (cf >= 0) & (cf < NC)
        on_b = (cb >= 0) & (cb < NC)

        @pl.when(s < NC)
        def _():
            local(s)

        @pl.when(on_f)
        def _():
            fwd_pass(cf)

        @pl.when(on_b)
        def _():
            bwd_pass(cb)

        @pl.when(on_f)
        def _():
            fwd_finish(cf)

        @pl.when(on_b)
        def _():
            bwd_finish(cb)

        @pl.when(cs == 0)
        def _():
            soft_begin()

        @pl.when((cs >= 0) & (cs < NC))
        def _():
            soft(cs)

        return carry

    lax.fori_loop(0, NC + max(LAG * (n - 1), SOFT_DELAY), step, 0)

    for g in range(G):
        at = slice(g * D, (g + 1) * D)
        for slot in range(2):

            @pl.when(there(slot + 1))
            def _():
                grad_copy(slot, g).wait_recv()

        sk_out[:, at] = (acc[0, g, 0] + gland[0, g, 0] + gland[1, g, 0]).astype(BF16)
        sv_out[:, at] = (acc[0, g, 1] + gland[0, g, 1] + gland[1, g, 1]).astype(BF16)

    def drain(c, carry):
        @pl.when(there(1))
        def _():
            fwd_copy(c).wait_send()

        @pl.when(there(-1))
        def _():
            bwd_copy(c).wait_send()

        return carry

    lax.fori_loop(0, NC, drain, 0)
    for slot in range(2):

        @pl.when(there(slot + 1))
        def _():
            kv_copy(slot, 0).wait_send()
            kv_copy(slot, 1).wait_send()

        @pl.when(there(-slot - 1))
        def _():
            for g in range(G):
                grad_copy(slot, g).wait_send()


def body(q, k, v, do, power, surplus, sq, sk, sv, sdo):
    n = lax.axis_size("ctx")
    T, HD = q.shape
    H = surplus.shape[1]
    D = HD // H
    NC = H // CH
    rate = surplus - jnp.power(2.0, -power.astype(F32))[None, :]
    cum = jnp.cumsum(rate, axis=0).T.reshape(H, 1, T)
    whole = jax.ShapeDtypeStruct((T, HD), BF16)
    narrow = jax.ShapeDtypeStruct(sk.shape, BF16)
    vm = pl.BlockSpec(memory_space=pltpu.VMEM)
    dma = pltpu.SemaphoreType.DMA
    return pl.pallas_call(
        functools.partial(kernel, n),
        out_shape=(whole, whole, whole, whole, narrow, narrow),
        in_specs=[vm] * 9,
        out_specs=[vm] * 6,
        scratch_shapes=[
            pltpu.VMEM((H, T, T), BF16),
            pltpu.VMEM((H, T, T), BF16),
            pltpu.VMEM((H, D, D), F32),
            pltpu.VMEM((H, D, D), F32),
            pltpu.VMEM((H, D, D), BF16),
            pltpu.VMEM((H, D, D), BF16),
            pltpu.VMEM((H, D, D), BF16),
            pltpu.VMEM((H, D, D), BF16),
            pltpu.VMEM((2, 2) + sk.shape, BF16),
            pltpu.VMEM((G, WINDOW * T, D), BF16),
            pltpu.VMEM((G, WINDOW * T, D), BF16),
            pltpu.VMEM((WINDOW, G, 2, T, D), F32),
            pltpu.VMEM((2, G, 2, T, D), F32),
            dma((NC,)),
            dma((NC,)),
            dma((NC,)),
            dma((NC,)),
            dma((4,)),
            dma((4,)),
            dma((2, G)),
            dma((2, G)),
        ],
        compiler_params=pltpu.CompilerParams(
            collective_id=0, has_side_effects=True, vmem_limit_bytes=48 * 1024 * 1024
        ),
        cost_estimate=pl.CostEstimate(
            flops=4_000_000_000, bytes_accessed=12_000_000, transcendentals=4_000_000
        ),
    )(q, k, v, do, cum, sq, sk, sv, sdo)


def solution(mesh):
    rows = P(("dp", "ctx"), None)
    return jax.shard_map(
        body,
        mesh=mesh,
        in_specs=(rows, rows, rows, rows, P("dp"), rows, rows, rows, rows, rows),
        out_specs=(rows,) * 6,
        check_vma=False,
    )
```

```python
import functools

import jax
import jax.numpy as jnp
from jax import lax
from jax.experimental import pallas as pl
from jax.experimental.pallas import tpu as pltpu
from jax.sharding import PartitionSpec as P

G = 4
WINDOW = 3
CH = 2
LAG = 2
FINISH_CH = 4
SOFT_CH = 2
SOFT_DELAY = 8
SOFT_EVERY = 1
F32 = jnp.float32
BF16 = jnp.bfloat16


def dot(a, b, ca, cb):
    return lax.dot_general(a, b, (((ca,), (cb,)), ((), ())), preferred_element_type=F32)


def kernel(
    n,
    q_ref,
    k_ref,
    v_ref,
    do_ref,
    cum_ref,
    sq_ref,
    sk_ref,
    sv_ref,
    sdo_ref,
    lq_out,
    lk_out,
    lv_out,
    sq_out,
    sk_out,
    sv_out,
    rise_s,
    fall_s,
    tall_s,
    ks_s,
    gs_s,
    fin,
    fout,
    gin,
    gout,
    kvin,
    kcat,
    vcat,
    acc,
    gsent,
    gland,
    fsend,
    frecv,
    bsend,
    brecv,
    kvsend,
    kvrecv,
    gsend,
    grecv,
):
    T = q_ref.shape[0]
    D = T
    H = cum_ref.shape[0]
    NC = H // CH
    share = H // G
    per_group = share // SOFT_CH
    NU = H // SOFT_CH
    me = lax.axis_index("ctx")
    scale = 1.0 / D
    sscale = D ** (-0.5)

    def there(offset):
        return (me + offset >= 0) & (me + offset < n)

    def device(offset):
        if offset > 0:
            return {"ctx": jnp.where(me + offset < n, me + offset, me - offset)}
        return {"ctx": jnp.where(me + offset >= 0, me + offset, me - offset)}

    def remote(src, dst, send, recv, offset):
        return pltpu.make_async_remote_copy(
            src_ref=src,
            dst_ref=dst,
            send_sem=send,
            recv_sem=recv,
            device_id=device(offset),
            device_id_type=pl.DeviceIdType.MESH,
        )

    def fwd_copy(c):
        part = pl.ds(c * CH, CH)
        return remote(fout.at[part], fin.at[part], fsend.at[c], frecv.at[c], 1)

    def bwd_copy(c):
        part = pl.ds(c * CH, CH)
        return remote(gout.at[part], gin.at[part], bsend.at[c], brecv.at[c], -1)

    def kv_copy(slot, which):
        src = sk_ref if which == 0 else sv_ref
        i = slot * 2 + which
        return remote(src, kvin.at[slot, which], kvsend.at[i], kvrecv.at[i], slot + 1)

    def grad_copy(slot, g):
        return remote(
            gsent.at[slot, g], gland.at[slot, g], gsend.at[slot, g], grecv.at[slot, g], -(slot + 1)
        )

    barrier = pltpu.get_barrier_semaphore()
    for offset in (-2, -1, 1, 2):

        @pl.when(there(offset))
        def _():
            pl.semaphore_signal(
                barrier, inc=1, device_id=device(offset), device_id_type=pl.DeviceIdType.MESH
            )

    peers = jnp.minimum(me, 2) + jnp.minimum(n - 1 - me, 2)
    pl.semaphore_wait(barrier, peers)

    for slot in range(2):

        @pl.when(there(slot + 1))
        def _():
            kv_copy(slot, 0).start()
            kv_copy(slot, 1).start()

        @pl.when(jnp.logical_not(there(-slot - 1)))
        def _():
            kvin[slot] = jnp.zeros(kvin.shape[1:], BF16)

        @pl.when(jnp.logical_not(there(slot + 1)))
        def _():
            gland[slot] = jnp.zeros(gland.shape[1:], BF16)

    @pl.when(me == 0)
    def _():
        fin[...] = jnp.zeros(fin.shape, BF16)

    @pl.when(me == n - 1)
    def _():
        gin[...] = jnp.zeros(gin.shape, BF16)

    acc[...] = jnp.zeros(acc.shape, F32)

    rows_i = lax.broadcasted_iota(jnp.int32, (T, T), 0)
    cols_i = lax.broadcasted_iota(jnp.int32, (T, T), 1)

    def cols(h):
        return pl.ds(pl.multiple_of(h * D, D), D)

    def local(c):
        for j in range(CH):
            h = c * CH + j
            at = cols(h)
            row = cum_ref[h]
            tall = jnp.broadcast_to(row, (T, T)).T
            rise = jnp.exp(tall)
            fall = jnp.exp(row[:, T - 1 : T] - tall)
            tall_s[h] = tall
            rise_s[h] = rise
            fall_s[h] = fall
            wk = (k_ref[:, at].astype(F32) * fall).astype(BF16)
            wq = (q_ref[:, at].astype(F32) * rise).astype(BF16)
            ks_s[h] = dot(wk, v_ref[:, at], 0, 0)
            gs_s[h] = dot(wq, do_ref[:, at], 0, 0)

    def pass_state(c, state, arrived, out):
        for j in range(CH):
            h = c * CH + j
            row = cum_ref[h]
            out[h] = (state[h] + jnp.exp(row[:, T - 1 : T]) * arrived[h].astype(F32)).astype(BF16)

    def fwd_pass(c):
        @pl.when(there(-1))
        def _():
            fwd_copy(c).wait_recv()

        @pl.when(there(1))
        def _():
            pass_state(c, ks_s, fin, fout)
            fwd_copy(c).start()

    def bwd_pass(c):
        @pl.when(there(1))
        def _():
            bwd_copy(c).wait_recv()

        @pl.when(there(-1))
        def _():
            pass_state(c, gs_s, gin, gout)
            bwd_copy(c).start()

    def finish(f):
        results = []
        for j in range(FINISH_CH):
            h = f * FINISH_CH + j
            at = cols(h)
            q, k, v, do = q_ref[:, at], k_ref[:, at], v_ref[:, at], do_ref[:, at]
            key_in, grad_in = fin[h], gin[h]
            fade = jnp.exp(jnp.minimum(tall_s[h] - cum_ref[h], 0.0))
            decay = jnp.where(rows_i >= cols_i, fade, 0.0) * scale
            mg = (decay * dot(do, v, 1, 1)).astype(BF16)
            ms = (decay * dot(q, k, 1, 1)).astype(BF16)
            rise = rise_s[h] * scale
            fall = fall_s[h] * scale
            results.append(
                (
                    at,
                    (dot(mg, k, 1, 0) + rise * dot(do, key_in, 1, 1)).astype(BF16),
                    (dot(mg, q, 0, 0) + fall * dot(v, grad_in, 1, 1)).astype(BF16),
                    (dot(ms, do, 0, 0) + fall * dot(k, grad_in, 1, 0)).astype(BF16),
                )
            )
        for at, a, b, c in results:
            lq_out[:, at] = a
            lk_out[:, at] = b
            lv_out[:, at] = c

    def soft_begin():
        for slot in range(2):

            @pl.when(there(-slot - 1))
            def _():
                kv_copy(slot, 0).wait_recv()
                kv_copy(slot, 1).wait_recv()

        for g in range(G):
            at = slice(g * D, (g + 1) * D)
            kcat[g, 0:T] = sk_ref[:, at]
            vcat[g, 0:T] = sv_ref[:, at]
            for slot in range(2):
                kcat[g, (slot + 1) * T : (slot + 2) * T] = kvin[slot, 0, :, at]
                vcat[g, (slot + 1) * T : (slot + 2) * T] = kvin[slot, 1, :, at]

    span = WINDOW * T

    def soft(c):
        g = c // per_group
        k, v = kcat[g], vcat[g]
        q = jnp.concatenate([sq_ref[:, cols(c * SOFT_CH + j)] for j in range(SOFT_CH)], axis=0)
        do = jnp.concatenate([sdo_ref[:, cols(c * SOFT_CH + j)] for j in range(SOFT_CH)], axis=0)
        t = lax.broadcasted_iota(jnp.int32, (SOFT_CH * T, span), 0) % T
        s = lax.broadcasted_iota(jnp.int32, (SOFT_CH * T, span), 1)
        visible = (s <= t) | ((s >= T) & (s < (me + 1) * T))
        score = jnp.where(visible, dot(q, k, 1, 1) * sscale, -jnp.inf)
        peak = jnp.max(score, axis=1, keepdims=True)
        expo = jnp.exp(score - peak)
        prob = expo * (1.0 / jnp.sum(expo, axis=1, keepdims=True))
        half = prob.astype(BF16)
        out = dot(half, v, 1, 0).astype(BF16)
        delta = jnp.sum(do.astype(F32) * out.astype(F32), axis=1, keepdims=True)
        ds = (prob * (dot(do, v, 1, 1) - delta)).astype(BF16)
        dq = (dot(ds, k, 1, 0) * sscale).astype(BF16)
        for j in range(SOFT_CH):
            sq_out[:, cols(c * SOFT_CH + j)] = dq[j * T : (j + 1) * T]
        dk = dot(ds, q, 0, 0) * sscale
        dv = dot(half, do, 0, 0)
        for slot in range(WINDOW):
            acc[slot, g, 0] += dk[slot * T : (slot + 1) * T]
            acc[slot, g, 1] += dv[slot * T : (slot + 1) * T]

        @pl.when(c % per_group == per_group - 1)
        def _():
            for slot in range(2):

                @pl.when(there(-slot - 1))
                def _():
                    gsent[slot, g] = acc[slot + 1, g].astype(BF16)
                    grad_copy(slot, g).start()

    RATIO = FINISH_CH // CH

    def step(s, carry):
        cf = s - LAG * me
        cb = s - LAG * (n - 1 - me)
        cs = s - SOFT_DELAY
        unit = cs // SOFT_EVERY
        on_f = (cf >= 0) & (cf < NC)
        on_b = (cb >= 0) & (cb < NC)

        @pl.when(s < NC)
        def _():
            local(s)

        @pl.when(on_f)
        def _():
            fwd_pass(cf)

        @pl.when(on_b)
        def _():
            bwd_pass(cb)

        last = s - LAG * jnp.maximum(me, n - 1 - me)
        unit_f = last // RATIO

        @pl.when((last >= 0) & (last % RATIO == RATIO - 1) & (last < NC))
        def _():
            finish(unit_f)

        @pl.when(cs == 0)
        def _():
            soft_begin()

        @pl.when((cs >= 0) & (cs % SOFT_EVERY == 0) & (unit < NU))
        def _():
            soft(unit)

        return carry

    lax.fori_loop(0, max(NC + LAG * (n - 1), SOFT_DELAY + SOFT_EVERY * (NU - 1) + 1), step, 0)

    for g in range(G):
        at = slice(g * D, (g + 1) * D)
        for slot in range(2):

            @pl.when(there(slot + 1))
            def _():
                grad_copy(slot, g).wait_recv()

        later = gland[0, g, 0].astype(F32) + gland[1, g, 0].astype(F32)
        sk_out[:, at] = (acc[0, g, 0] + later).astype(BF16)
        later = gland[0, g, 1].astype(F32) + gland[1, g, 1].astype(F32)
        sv_out[:, at] = (acc[0, g, 1] + later).astype(BF16)

    def drain(c, carry):
        @pl.when(there(1))
        def _():
            fwd_copy(c).wait_send()

        @pl.when(there(-1))
        def _():
            bwd_copy(c).wait_send()

        return carry

    lax.fori_loop(0, NC, drain, 0)
    for slot in range(2):

        @pl.when(there(slot + 1))
        def _():
            kv_copy(slot, 0).wait_send()
            kv_copy(slot, 1).wait_send()

        @pl.when(there(-slot - 1))
        def _():
            for g in range(G):
                grad_copy(slot, g).wait_send()


def body(q, k, v, do, power, surplus, sq, sk, sv, sdo):
    n = lax.axis_size("ctx")
    T, HD = q.shape
    H = surplus.shape[1]
    D = HD // H
    NC = H // CH
    rate = surplus - jnp.power(2.0, -power.astype(F32))[None, :]
    cum = jnp.cumsum(rate, axis=0).T.reshape(H, 1, T)
    whole = jax.ShapeDtypeStruct((T, HD), BF16)
    narrow = jax.ShapeDtypeStruct(sk.shape, BF16)
    vm = pl.BlockSpec(memory_space=pltpu.VMEM)
    dma = pltpu.SemaphoreType.DMA
    return pl.pallas_call(
        functools.partial(kernel, n),
        out_shape=(whole, whole, whole, whole, narrow, narrow),
        in_specs=[vm] * 9,
        out_specs=[vm] * 6,
        scratch_shapes=[
            pltpu.VMEM((H, T, T), F32),
            pltpu.VMEM((H, T, T), F32),
            pltpu.VMEM((H, T, T), F32),
            pltpu.VMEM((H, D, D), F32),
            pltpu.VMEM((H, D, D), F32),
            pltpu.VMEM((H, D, D), BF16),
            pltpu.VMEM((H, D, D), BF16),
            pltpu.VMEM((H, D, D), BF16),
            pltpu.VMEM((H, D, D), BF16),
            pltpu.VMEM((2, 2) + sk.shape, BF16),
            pltpu.VMEM((G, WINDOW * T, D), BF16),
            pltpu.VMEM((G, WINDOW * T, D), BF16),
            pltpu.VMEM((WINDOW, G, 2, T, D), F32),
            pltpu.VMEM((2, G, 2, T, D), BF16),
            pltpu.VMEM((2, G, 2, T, D), BF16),
            dma((NC,)),
            dma((NC,)),
            dma((NC,)),
            dma((NC,)),
            dma((4,)),
            dma((4,)),
            dma((2, G)),
            dma((2, G)),
        ],
        compiler_params=pltpu.CompilerParams(
            collective_id=0, has_side_effects=True, vmem_limit_bytes=48 * 1024 * 1024
        ),
        cost_estimate=pl.CostEstimate(
            flops=4_000_000_000, bytes_accessed=12_000_000, transcendentals=4_000_000
        ),
    )(q, k, v, do, cum, sq, sk, sv, sdo)


def solution(mesh):
    rows = P(("dp", "ctx"), None)
    return jax.shard_map(
        body,
        mesh=mesh,
        in_specs=(rows, rows, rows, rows, P("dp"), rows, rows, rows, rows, rows),
        out_specs=(rows,) * 6,
        check_vma=False,
    )
```

```python
import functools

import jax
import jax.numpy as jnp
from jax import lax
from jax.experimental import pallas as pl
from jax.experimental.pallas import tpu as pltpu
from jax.sharding import PartitionSpec as P

G = 4
WINDOW = 3
CH = 1
LAG = 4
FINISH_CH = 4
SOFT_CH = 2
SOFT_DELAY = 20
SOFT_EVERY = 2
F32 = jnp.float32
BF16 = jnp.bfloat16


def dot(a, b, ca, cb):
    return lax.dot_general(a, b, (((ca,), (cb,)), ((), ())), preferred_element_type=F32)


def kernel(
    n,
    q_ref,
    k_ref,
    v_ref,
    do_ref,
    cum_ref,
    sq_ref,
    sk_ref,
    sv_ref,
    sdo_ref,
    lq_out,
    lk_out,
    lv_out,
    sq_out,
    sk_out,
    sv_out,
    rise_s,
    fall_s,
    tall_s,
    ks_s,
    gs_s,
    fin,
    fout,
    gin,
    gout,
    kvin,
    kcat,
    vcat,
    acc,
    gsent,
    gland,
    fsend,
    frecv,
    bsend,
    brecv,
    kvsend,
    kvrecv,
    gsend,
    grecv,
):
    T = q_ref.shape[0]
    D = T
    H = cum_ref.shape[0]
    NC = H // CH
    share = H // G
    per_group = share // SOFT_CH
    NU = H // SOFT_CH
    me = lax.axis_index("ctx")
    scale = 1.0 / D
    sscale = D ** (-0.5)

    def there(offset):
        return (me + offset >= 0) & (me + offset < n)

    def device(offset):
        if offset > 0:
            return {"ctx": jnp.where(me + offset < n, me + offset, me - offset)}
        return {"ctx": jnp.where(me + offset >= 0, me + offset, me - offset)}

    def remote(src, dst, send, recv, offset):
        return pltpu.make_async_remote_copy(
            src_ref=src,
            dst_ref=dst,
            send_sem=send,
            recv_sem=recv,
            device_id=device(offset),
            device_id_type=pl.DeviceIdType.MESH,
        )

    def fwd_copy(c):
        part = pl.ds(c * CH, CH)
        return remote(fout.at[part], fin.at[part], fsend.at[c], frecv.at[c], 1)

    def bwd_copy(c):
        part = pl.ds(c * CH, CH)
        return remote(gout.at[part], gin.at[part], bsend.at[c], brecv.at[c], -1)

    def kv_copy(slot, which):
        src = sk_ref if which == 0 else sv_ref
        i = slot * 2 + which
        return remote(src, kvin.at[slot, which], kvsend.at[i], kvrecv.at[i], slot + 1)

    def grad_copy(slot, g):
        return remote(
            gsent.at[slot, g], gland.at[slot, g], gsend.at[slot, g], grecv.at[slot, g], -(slot + 1)
        )

    barrier = pltpu.get_barrier_semaphore()
    for offset in (-2, -1, 1, 2):

        @pl.when(there(offset))
        def _():
            pl.semaphore_signal(
                barrier, inc=1, device_id=device(offset), device_id_type=pl.DeviceIdType.MESH
            )

    peers = jnp.minimum(me, 2) + jnp.minimum(n - 1 - me, 2)
    pl.semaphore_wait(barrier, peers)

    for slot in range(2):

        @pl.when(there(slot + 1))
        def _():
            kv_copy(slot, 0).start()
            kv_copy(slot, 1).start()

        @pl.when(jnp.logical_not(there(-slot - 1)))
        def _():
            kvin[slot] = jnp.zeros(kvin.shape[1:], BF16)

        @pl.when(jnp.logical_not(there(slot + 1)))
        def _():
            gland[slot] = jnp.zeros(gland.shape[1:], BF16)

    @pl.when(me == 0)
    def _():
        fin[...] = jnp.zeros(fin.shape, BF16)

    @pl.when(me == n - 1)
    def _():
        gin[...] = jnp.zeros(gin.shape, BF16)

    acc[...] = jnp.zeros(acc.shape, F32)

    rows_i = lax.broadcasted_iota(jnp.int32, (T, T), 0)
    cols_i = lax.broadcasted_iota(jnp.int32, (T, T), 1)

    def cols(h):
        return pl.ds(pl.multiple_of(h * D, D), D)

    def local(c):
        for j in range(CH):
            h = c * CH + j
            at = cols(h)
            row = cum_ref[h]
            tall = jnp.broadcast_to(row, (T, T)).T
            rise = jnp.exp(tall)
            fall = jnp.exp(row[:, T - 1 : T] - tall)
            tall_s[h] = tall
            rise_s[h] = rise
            fall_s[h] = fall
            wk = (k_ref[:, at].astype(F32) * fall).astype(BF16)
            wq = (q_ref[:, at].astype(F32) * rise).astype(BF16)
            ks_s[h] = dot(wk, v_ref[:, at], 0, 0)
            gs_s[h] = dot(wq, do_ref[:, at], 0, 0)

    def pass_state(c, state, arrived, out):
        for j in range(CH):
            h = c * CH + j
            row = cum_ref[h]
            out[h] = (state[h] + jnp.exp(row[:, T - 1 : T]) * arrived[h].astype(F32)).astype(BF16)

    def fwd_pass(c):
        @pl.when(there(-1))
        def _():
            fwd_copy(c).wait_recv()

        @pl.when(there(1))
        def _():
            pass_state(c, ks_s, fin, fout)
            fwd_copy(c).start()

    def bwd_pass(c):
        @pl.when(there(1))
        def _():
            bwd_copy(c).wait_recv()

        @pl.when(there(-1))
        def _():
            pass_state(c, gs_s, gin, gout)
            bwd_copy(c).start()

    def finish(f):
        results = []
        for j in range(FINISH_CH):
            h = f * FINISH_CH + j
            at = cols(h)
            q, k, v, do = q_ref[:, at], k_ref[:, at], v_ref[:, at], do_ref[:, at]
            key_in, grad_in = fin[h], gin[h]
            fade = jnp.exp(jnp.minimum(tall_s[h] - cum_ref[h], 0.0))
            decay = jnp.where(rows_i >= cols_i, fade, 0.0) * scale
            mg = (decay * dot(do, v, 1, 1)).astype(BF16)
            ms = (decay * dot(q, k, 1, 1)).astype(BF16)
            rise = rise_s[h] * scale
            fall = fall_s[h] * scale
            results.append(
                (
                    at,
                    (dot(mg, k, 1, 0) + rise * dot(do, key_in, 1, 1)).astype(BF16),
                    (dot(mg, q, 0, 0) + fall * dot(v, grad_in, 1, 1)).astype(BF16),
                    (dot(ms, do, 0, 0) + fall * dot(k, grad_in, 1, 0)).astype(BF16),
                )
            )
        for at, a, b, c in results:
            lq_out[:, at] = a
            lk_out[:, at] = b
            lv_out[:, at] = c

    def soft_begin():
        for slot in range(2):

            @pl.when(there(-slot - 1))
            def _():
                kv_copy(slot, 0).wait_recv()
                kv_copy(slot, 1).wait_recv()

        for g in range(G):
            at = slice(g * D, (g + 1) * D)
            kcat[g, 0:T] = sk_ref[:, at]
            vcat[g, 0:T] = sv_ref[:, at]
            for slot in range(2):
                kcat[g, (slot + 1) * T : (slot + 2) * T] = kvin[slot, 0, :, at]
                vcat[g, (slot + 1) * T : (slot + 2) * T] = kvin[slot, 1, :, at]

    span = WINDOW * T

    def soft(c):
        g = c // per_group
        k, v = kcat[g], vcat[g]
        q = jnp.concatenate([sq_ref[:, cols(c * SOFT_CH + j)] for j in range(SOFT_CH)], axis=0)
        do = jnp.concatenate([sdo_ref[:, cols(c * SOFT_CH + j)] for j in range(SOFT_CH)], axis=0)
        t = lax.broadcasted_iota(jnp.int32, (SOFT_CH * T, span), 0) % T
        s = lax.broadcasted_iota(jnp.int32, (SOFT_CH * T, span), 1)
        visible = (s <= t) | ((s >= T) & (s < (me + 1) * T))
        score = jnp.where(visible, dot(q, k, 1, 1) * sscale, -jnp.inf)
        peak = jnp.max(score, axis=1, keepdims=True)
        expo = jnp.exp(score - peak)
        prob = expo * (1.0 / jnp.sum(expo, axis=1, keepdims=True))
        half = prob.astype(BF16)
        out = dot(half, v, 1, 0).astype(BF16)
        delta = jnp.sum(do.astype(F32) * out.astype(F32), axis=1, keepdims=True)
        ds = (prob * (dot(do, v, 1, 1) - delta)).astype(BF16)
        dq = (dot(ds, k, 1, 0) * sscale).astype(BF16)
        for j in range(SOFT_CH):
            sq_out[:, cols(c * SOFT_CH + j)] = dq[j * T : (j + 1) * T]
        dk = dot(ds, q, 0, 0) * sscale
        dv = dot(half, do, 0, 0)
        for slot in range(WINDOW):
            acc[slot, g, 0] += dk[slot * T : (slot + 1) * T]
            acc[slot, g, 1] += dv[slot * T : (slot + 1) * T]

        @pl.when(c % per_group == per_group - 1)
        def _():
            for slot in range(2):

                @pl.when(there(-slot - 1))
                def _():
                    gsent[slot, g] = acc[slot + 1, g].astype(BF16)
                    grad_copy(slot, g).start()

    RATIO = FINISH_CH // CH

    def step(s, carry):
        cf = s - LAG * me
        cb = s - LAG * (n - 1 - me)
        cs = s - SOFT_DELAY
        unit = cs // SOFT_EVERY
        on_f = (cf >= 0) & (cf < NC)
        on_b = (cb >= 0) & (cb < NC)

        @pl.when(s < NC)
        def _():
            local(s)

        @pl.when(on_f)
        def _():
            fwd_pass(cf)

        @pl.when(on_b)
        def _():
            bwd_pass(cb)

        last = s - LAG * jnp.maximum(me, n - 1 - me)
        unit_f = last // RATIO

        @pl.when((last >= 0) & (last % RATIO == RATIO - 1) & (last < NC))
        def _():
            finish(unit_f)

        @pl.when(cs == 0)
        def _():
            soft_begin()

        @pl.when((cs >= 0) & (cs % SOFT_EVERY == 0) & (unit < NU))
        def _():
            soft(unit)

        return carry

    lax.fori_loop(0, max(NC + LAG * (n - 1), SOFT_DELAY + SOFT_EVERY * (NU - 1) + 1), step, 0)

    for g in range(G):
        at = slice(g * D, (g + 1) * D)
        for slot in range(2):

            @pl.when(there(slot + 1))
            def _():
                grad_copy(slot, g).wait_recv()

        later = gland[0, g, 0].astype(F32) + gland[1, g, 0].astype(F32)
        sk_out[:, at] = (acc[0, g, 0] + later).astype(BF16)
        later = gland[0, g, 1].astype(F32) + gland[1, g, 1].astype(F32)
        sv_out[:, at] = (acc[0, g, 1] + later).astype(BF16)

    def drain(c, carry):
        @pl.when(there(1))
        def _():
            fwd_copy(c).wait_send()

        @pl.when(there(-1))
        def _():
            bwd_copy(c).wait_send()

        return carry

    lax.fori_loop(0, NC, drain, 0)
    for slot in range(2):

        @pl.when(there(slot + 1))
        def _():
            kv_copy(slot, 0).wait_send()
            kv_copy(slot, 1).wait_send()

        @pl.when(there(-slot - 1))
        def _():
            for g in range(G):
                grad_copy(slot, g).wait_send()


def body(q, k, v, do, power, surplus, sq, sk, sv, sdo):
    n = lax.axis_size("ctx")
    T, HD = q.shape
    H = surplus.shape[1]
    D = HD // H
    NC = H // CH
    rate = surplus - jnp.power(2.0, -power.astype(F32))[None, :]
    cum = jnp.cumsum(rate, axis=0).T.reshape(H, 1, T)
    whole = jax.ShapeDtypeStruct((T, HD), BF16)
    narrow = jax.ShapeDtypeStruct(sk.shape, BF16)
    vm = pl.BlockSpec(memory_space=pltpu.VMEM)
    dma = pltpu.SemaphoreType.DMA
    return pl.pallas_call(
        functools.partial(kernel, n),
        out_shape=(whole, whole, whole, whole, narrow, narrow),
        in_specs=[vm] * 9,
        out_specs=[vm] * 6,
        scratch_shapes=[
            pltpu.VMEM((H, T, T), F32),
            pltpu.VMEM((H, T, T), F32),
            pltpu.VMEM((H, T, T), F32),
            pltpu.VMEM((H, D, D), F32),
            pltpu.VMEM((H, D, D), F32),
            pltpu.VMEM((H, D, D), BF16),
            pltpu.VMEM((H, D, D), BF16),
            pltpu.VMEM((H, D, D), BF16),
            pltpu.VMEM((H, D, D), BF16),
            pltpu.VMEM((2, 2) + sk.shape, BF16),
            pltpu.VMEM((G, WINDOW * T, D), BF16),
            pltpu.VMEM((G, WINDOW * T, D), BF16),
            pltpu.VMEM((WINDOW, G, 2, T, D), F32),
            pltpu.VMEM((2, G, 2, T, D), BF16),
            pltpu.VMEM((2, G, 2, T, D), BF16),
            dma((NC,)),
            dma((NC,)),
            dma((NC,)),
            dma((NC,)),
            dma((4,)),
            dma((4,)),
            dma((2, G)),
            dma((2, G)),
        ],
        compiler_params=pltpu.CompilerParams(
            collective_id=0, has_side_effects=True, vmem_limit_bytes=48 * 1024 * 1024
        ),
        cost_estimate=pl.CostEstimate(
            flops=4_000_000_000, bytes_accessed=12_000_000, transcendentals=4_000_000
        ),
    )(q, k, v, do, cum, sq, sk, sv, sdo)


def solution(mesh):
    rows = P(("dp", "ctx"), None)
    return jax.shard_map(
        body,
        mesh=mesh,
        in_specs=(rows, rows, rows, rows, P("dp"), rows, rows, rows, rows, rows),
        out_specs=(rows,) * 6,
        check_vma=False,
    )
```
